512 devices in a mesh: tok: 16 (over z, core), voc: 32 (over x, y).
Axes of the slice: x: 4, y: 8, z: 8, core: 2. Of those that a mesh axis runs over, the one named last changes fastest.
Arguments:
- hidden: bfloat16 [8192, 3584], P('tok', 'voc'), may hold values from -30 to 30
- unembed: bfloat16 [3584, 8192], P(None, 'voc'), may hold values from -1 to 1
- teacher: bfloat16 [8192, 8192], P('tok', 'voc'), may hold values from -12 to 12
- teacher_lse: float32 [8192], P('tok'), may hold values from 14 to 18
- cotangent: float32 [8192], P('tok'), may hold values from -4 to 4
Outputs:
- loss: float32 [8192], P('tok')
- grad_hidden: bfloat16 [8192, 3584], P('tok', 'voc')
- grad_unembed: bfloat16 [3584, 8192], P(None, 'voc')
The draws below stay inside these ranges and needn't reach their ends.
All inputs are finite; a program needn't handle non-finite values.
Results may differ from the reference program's by a relative error of at most 0.023.
Values may be sent and summed in bfloat16 or wider, within the bound.
No kernel may reach another device: no remote copies, remote signals or barrier semaphores. Data moves between devices by JAX's collectives and lax.ppermute only.
A program may use at most 64 MiB of HBM per device.

```python
import math
import jax
import jax.numpy as jnp
from jax import lax

D = 3584
TOK_DEV = 512
VC_DEV = 256
TOKENS = 8192
V = 8192
N_TOK = 16
N_VOC = 32


def unembed_table(key, signed):
    if signed:
        values = jax.random.rademacher(key, (D, V), jnp.int32).astype(jnp.float32)
    else:
        values = jnp.clip(jax.random.normal(key, (D, V), jnp.float32), -6.0, 6.0)
    return values * D ** (-0.5)


def draw_unembed(key, part):
    table = unembed_table(key, False)
    return table.astype(jnp.bfloat16)


def draw_hidden(key, part):
    key = jax.random.fold_in(key, 7)
    key_noise, key_scale = jax.random.split(key, 2)
    scales = jnp.exp(jax.random.uniform(key_scale, (TOKENS, 1), jnp.float32, 0.0, math.log(10.0)))
    noise = jnp.clip(jax.random.normal(key_noise, (TOKENS, D), jnp.float32), -3.0, 3.0)
    values = noise * scales
    return jnp.clip(values, -30.0, 30.0).astype(jnp.bfloat16)


def draw_teacher(key, part):
    key = jax.random.fold_in(key, 11)
    key_noise = jax.random.fold_in(key, 0)
    column_bias = 1.1 * jnp.arange(V, dtype=jnp.float32)[None, :] / V
    noise = 3.0 * jnp.clip(jax.random.normal(key_noise, (TOKENS, V), jnp.float32), -3.4, 3.4)
    return jnp.clip(noise + column_bias, -12.0, 12.0).astype(jnp.bfloat16)


def block_scale(key, dims, cuts, least, top_value):
    loudness, own = 1.0, jax.random.fold_in(key, 6)
    for axis_at, shards_of in cuts:
        heights = jnp.exp(jax.random.uniform(jax.random.fold_in(own, axis_at), (shards_of,), jnp.float32, least / len(cuts), top_value / len(cuts)))
        loudness = loudness * jnp.repeat(heights, dims[axis_at] // shards_of).reshape([-1 if axis == axis_at else 1 for axis in range(len(dims))])
    return loudness


def bell_draw(own_key, shape, deviation, most, shards=(), kind=jnp.bfloat16):
    entries = jax.random.normal(own_key, shape, jnp.float32) * deviation
    if len(shards) > 0:
        entries = block_scale(own_key, shape, shards, -0.22, 0.18) * entries
    return jnp.clip(entries, min=-most, max=most).astype(kind)


def setup_inputs(seed: int = 0) -> dict:
    arg_keys = jax.random.split(jax.random.key(seed), 6)
    hidden = draw_hidden(jax.random.fold_in(arg_keys[5], 71), 0)
    unembed = draw_unembed(jax.random.fold_in(arg_keys[5], 71), 0)
    teacher = draw_teacher(jax.random.fold_in(arg_keys[5], 71), 0)
    teacher_lse = jnp.clip(14.0 + 4.0 * jax.random.uniform(arg_keys[3], (TOKENS,), jnp.float32) ** block_scale(arg_keys[3], (TOKENS,), ((0, 16),), -0.2, 0.2), 14.0, 18.0)
    cotangent = bell_draw(arg_keys[4], (TOKENS,), 1.0, 4.0, ((0, 16),), jnp.float32)
    return {"hidden": hidden, "unembed": unembed, "teacher": teacher, "teacher_lse": teacher_lse, "cotangent": cotangent}


def reference(hidden, unembed, teacher, teacher_lse, cotangent):
    logits = jnp.dot(hidden, unembed, preferred_element_type=jnp.float32)
    row_top = jnp.max(logits, axis=1)
    student_lse = row_top + jnp.log(jnp.sum(jnp.exp(logits - row_top[:, None]), axis=1))
    teacher_f = teacher.astype(jnp.float32)
    probs = jnp.exp(teacher_f - teacher_lse[:, None])
    row_mass = jnp.sum(probs, axis=1)
    cross_term = jnp.sum(probs * (teacher_f - teacher_lse[:, None] - logits), axis=1)
    loss = cross_term + row_mass * student_lse
    grad_logits = (cotangent[:, None] * (jnp.exp(logits - student_lse[:, None]) * row_mass[:, None] - probs)).astype(jnp.bfloat16)

    def add_columns(block_index, total):
        start = jnp.asarray(block_index, jnp.int32) * VC_DEV
        grad_cols = lax.dynamic_slice_in_dim(grad_logits, start, VC_DEV, 1)
        weight_cols = lax.dynamic_slice_in_dim(unembed, start, VC_DEV, 1)
        partial_sum = lax.dot_general(grad_cols, weight_cols, (((1,), (1,)), ((), ())), preferred_element_type=jnp.float32)
        rounded = lax.optimization_barrier(partial_sum.astype(jnp.bfloat16))
        return total + rounded.astype(jnp.float32)

    grad_hidden = lax.fori_loop(0, N_VOC, add_columns, jnp.zeros((TOKENS, D), jnp.float32))

    def add_rows(block_index, total):
        start = jnp.asarray(block_index, jnp.int32) * TOK_DEV
        hidden_rows = lax.dynamic_slice_in_dim(hidden, start, TOK_DEV, 0)
        grad_rows = lax.dynamic_slice_in_dim(grad_logits, start, TOK_DEV, 0)
        partial_sum = lax.dot_general(hidden_rows, grad_rows, (((0,), (0,)), ((), ())), preferred_element_type=jnp.float32)
        rounded = lax.optimization_barrier(partial_sum.astype(jnp.bfloat16))
        return total + rounded.astype(jnp.float32)

    grad_unembed = lax.fori_loop(0, N_TOK, add_rows, jnp.zeros((D, V), jnp.float32))
    return loss, grad_hidden.astype(jnp.bfloat16), grad_unembed.astype(jnp.bfloat16)
```

```python
import jax
import jax.numpy as jnp
from jax import lax
from jax.sharding import PartitionSpec as P

NX, NY, NZ, NC = 4, 8, 8, 2
Y_GROUPS = [[x * NY + y for y in range(NY)] for x in range(NX)]
X_GROUPS = [[x * NY + y for x in range(NX)] for y in range(NY)]
Z_GROUPS = [[z * NC + c for z in range(NZ)] for c in range(NC)]
CORE_SWAP = [(z * NC + c, z * NC + 1 - c) for z in range(NZ) for c in range(NC)]


def exchange(blocks, axis, groups):
    return lax.all_to_all(blocks, axis, 0, 0, tiled=True, axis_index_groups=groups)


def spread(block, axis, groups):
    copies = jnp.broadcast_to(block[None], (len(groups[0]),) + block.shape)
    return exchange(copies, axis, groups)


def merge(parts):
    top = jnp.max(parts[:, 0], axis=0)
    total = jnp.sum(parts[:, 1] * jnp.exp(parts[:, 0] - top[None]), axis=0)
    return jnp.stack([top, total, jnp.sum(parts[:, 2], axis=0), jnp.sum(parts[:, 3], axis=0)])


def add_up(blocks):
    return jnp.sum(blocks.astype(jnp.float32), axis=0).astype(jnp.bfloat16)


def body(hidden, unembed, teacher, teacher_lse, cotangent):
    tokens, columns = teacher.shape
    features = unembed.shape[0]
    mine = hidden.T
    row = spread(mine, "voc", Y_GROUPS).reshape(NY * mine.shape[0], tokens)
    gathered = spread(row, "voc", X_GROUPS).reshape(features, tokens)

    teacher_t = teacher.T.astype(jnp.float32)
    shifted = teacher_t - teacher_lse[None, :]
    probs = jnp.exp(shifted)
    logits = lax.dot_general(
        unembed, gathered, (((0,), (0,)), ((), ())), preferred_element_type=jnp.float32
    )
    top = jnp.max(logits, axis=0)
    total = jnp.sum(jnp.exp(logits - top[None, :]), axis=0)
    mass = jnp.sum(probs, axis=0)
    cross = jnp.sum(probs * (shifted - logits), axis=0)
    stats = jnp.stack([top, total, mass, cross])
    stats = merge(spread(stats, "voc", Y_GROUPS))
    stats = merge(spread(stats, "voc", X_GROUPS))
    row_mass = stats[2]
    student_lse = stats[0] + jnp.log(stats[1])
    loss = stats[3] + row_mass * student_lse
    grad_logits = (
        cotangent[None, :] * (jnp.exp(logits - student_lse[None, :]) * row_mass[None, :] - probs)
    ).astype(jnp.bfloat16)

    weight_terms = lax.dot_general(
        gathered, grad_logits, (((1,), (1,)), ((), ())), preferred_element_type=jnp.float32
    ).astype(jnp.bfloat16)
    core = lax.rem(lax.axis_index("tok"), NC)
    half = features // NC
    kept = lax.dynamic_slice_in_dim(weight_terms, core * half, half, 0)
    given = lax.dynamic_slice_in_dim(weight_terms, (1 - core) * half, half, 0)
    came = lax.ppermute(given, "tok", CORE_SWAP)
    chip_terms = add_up(jnp.stack([kept, came])).reshape(NZ, half // NZ, columns)

    hidden_terms = jnp.dot(unembed, grad_logits, preferred_element_type=jnp.float32).astype(jnp.bfloat16)
    rows = add_up(exchange(hidden_terms.reshape(NX, features // NX, tokens), "voc", X_GROUPS))
    grad_hidden = add_up(exchange(rows.reshape(NY, features // NX // NY, tokens), "voc", Y_GROUPS)).T

    summed = add_up(exchange(chip_terms, "tok", Z_GROUPS))
    own_half = spread(summed, "tok", Z_GROUPS).reshape(half, columns)
    other_half = lax.ppermute(own_half, "tok", CORE_SWAP)
    low = jnp.where(core == 0, own_half, other_half)
    high = jnp.where(core == 0, other_half, own_half)
    return (loss, grad_hidden, jnp.concatenate([low, high], axis=0))


def solution(mesh):
    placed = (P("tok", "voc"), P(None, "voc"), P("tok", "voc"), P("tok"), P("tok"))
    return jax.shard_map(
        body,
        mesh=mesh,
        in_specs=placed,
        out_specs=(P("tok"), P("tok", "voc"), P(None, "voc")),
        check_vma=False,
    )
```

```python
import jax
import jax.numpy as jnp
from jax import lax
from jax.sharding import PartitionSpec as P

NX, NY, NZ, NC = 4, 8, 8, 2
Y_GROUPS = [[x * NY + y for y in range(NY)] for x in range(NX)]
X_GROUPS = [[x * NY + y for x in range(NX)] for y in range(NY)]
Z_GROUPS = [[z * NC + c for z in range(NZ)] for c in range(NC)]
CORE_SWAP = [(z * NC + c, z * NC + 1 - c) for z in range(NZ) for c in range(NC)]
ROWS_B = 64


def exchange(blocks, axis, groups):
    return lax.all_to_all(blocks, axis, 0, 0, tiled=True, axis_index_groups=groups)


def spread(block, axis, groups):
    copies = jnp.broadcast_to(block[None], (len(groups[0]),) + block.shape)
    return exchange(copies, axis, groups)


def merge(parts):
    top = jnp.max(parts[:, 0], axis=0)
    total = jnp.sum(parts[:, 1] * jnp.exp(parts[:, 0] - top[None]), axis=0)
    return jnp.stack([top, total, jnp.sum(parts[:, 2], axis=0), jnp.sum(parts[:, 3], axis=0)])


def add_up(blocks):
    return jnp.sum(blocks.astype(jnp.float32), axis=0).astype(jnp.bfloat16)


def contract(left, right, dims):
    return lax.dot_general(left, right, (dims, ((), ())), preferred_element_type=jnp.float32)


def body(hidden, unembed, teacher, teacher_lse, cotangent):
    tokens, columns = teacher.shape
    features = unembed.shape[0]
    shard = features // (NX * NY)
    rows_a = shard - ROWS_B
    mine = hidden.T

    line = spread(mine[:ROWS_B], "voc", X_GROUPS).reshape(NX * ROWS_B, tokens)
    gathered_b = lax.all_gather(line, "voc", axis_index_groups=Y_GROUPS, axis=0, tiled=True)
    part_a = lax.optimization_barrier((mine[ROWS_B:], line))[0]
    row = spread(part_a, "voc", Y_GROUPS).reshape(NY * rows_a, tokens)
    gathered_a = spread(row, "voc", X_GROUPS).reshape(NX * NY * rows_a, tokens)

    by_shard = unembed.reshape(NX, NY, shard, columns)
    unembed_b = by_shard[:, :, :ROWS_B].transpose(1, 0, 2, 3).reshape(-1, columns)
    unembed_a = by_shard[:, :, ROWS_B:].reshape(-1, columns)

    teacher_t = teacher.T.astype(jnp.float32)
    shifted = teacher_t - teacher_lse[None, :]
    probs = jnp.exp(shifted)
    logits = contract(unembed_b, gathered_b, ((0,), (0,))) + contract(unembed_a, gathered_a, ((0,), (0,)))
    top = jnp.max(logits, axis=0)
    total = jnp.sum(jnp.exp(logits - top[None, :]), axis=0)
    mass = jnp.sum(probs, axis=0)
    cross = jnp.sum(probs * (shifted - logits), axis=0)
    stats = jnp.stack([top, total, mass, cross])
    stats = merge(spread(stats, "voc", Y_GROUPS))
    stats = merge(spread(stats, "voc", X_GROUPS))
    row_mass = stats[2]
    student_lse = stats[0] + jnp.log(stats[1])
    loss = stats[3] + row_mass * student_lse
    grad_logits = (
        cotangent[None, :] * (jnp.exp(logits - student_lse[None, :]) * row_mass[None, :] - probs)
    ).astype(jnp.bfloat16)

    natural = jnp.concatenate(
        [
            gathered_b.reshape(NY, NX, ROWS_B, tokens).transpose(1, 0, 2, 3),
            gathered_a.reshape(NX, NY, rows_a, tokens),
        ],
        axis=2,
    ).reshape(NZ, NC, features // NZ // NC, tokens)
    core = lax.rem(lax.axis_index("tok"), NC)
    rows_kept = lax.dynamic_slice_in_dim(natural, core, 1, 1).reshape(-1, tokens)
    rows_given = lax.dynamic_slice_in_dim(natural, 1 - core, 1, 1).reshape(-1, tokens)
    given = contract(rows_given, grad_logits, ((1,), (1,))).astype(jnp.bfloat16)
    came = lax.ppermute(given, "tok", CORE_SWAP)

    terms_b = jnp.dot(unembed_b, grad_logits, preferred_element_type=jnp.float32).astype(jnp.bfloat16)
    line_b = lax.psum_scatter(
        terms_b, "voc", axis_index_groups=Y_GROUPS, scatter_dimension=0, tiled=True
    )
    chip_terms = (contract(rows_kept, grad_logits, ((1,), (1,))) + came.astype(jnp.float32)).astype(jnp.bfloat16)
    summed = add_up(exchange(chip_terms.reshape(NZ, -1, columns), "tok", Z_GROUPS))
    grad_unembed = lax.all_gather(summed, "tok", axis=0, tiled=True)

    terms_a = jnp.dot(unembed_a, grad_logits, preferred_element_type=jnp.float32).astype(jnp.bfloat16)
    row_a = add_up(exchange(terms_a.reshape(NX, -1, tokens), "voc", X_GROUPS))
    out_a = add_up(exchange(row_a.reshape(NY, -1, tokens), "voc", Y_GROUPS))
    out_b = add_up(exchange(line_b.reshape(NX, -1, tokens), "voc", X_GROUPS))
    grad_hidden = jnp.concatenate([out_b, out_a], axis=0).T
    return (loss, grad_hidden, grad_unembed)


def solution(mesh):
    placed = (P("tok", "voc"), P(None, "voc"), P("tok", "voc"), P("tok"), P("tok"))
    return jax.shard_map(
        body,
        mesh=mesh,
        in_specs=placed,
        out_specs=(P("tok"), P("tok", "voc"), P(None, "voc")),
        check_vma=False,
    )
```

```python
import jax
import jax.numpy as jnp
from jax import lax
from jax.sharding import PartitionSpec as P

NX, NY, NZ, NC = 4, 8, 8, 2
Y_GROUPS = [[x * NY + y for y in range(NY)] for x in range(NX)]
X_GROUPS = [[x * NY + y for x in range(NX)] for y in range(NY)]
Z_GROUPS = [[z * NC + c for z in range(NZ)] for c in range(NC)]
CORE_SWAP = [(z * NC + c, z * NC + 1 - c) for z in range(NZ) for c in range(NC)]
X_SHIFTS = [[(x * NY + y, (x + k) % NX * NY + y) for x in range(NX) for y in range(NY)] for k in range(NX)]
ROWS_B = 48


def exchange(blocks, axis, groups):
    return lax.all_to_all(blocks, axis, 0, 0, tiled=True, axis_index_groups=groups)


def spread(block, axis, groups):
    copies = jnp.broadcast_to(block[None], (len(groups[0]),) + block.shape)
    return exchange(copies, axis, groups)


def merge(parts):
    top = jnp.max(parts[:, 0], axis=0)
    total = jnp.sum(parts[:, 1] * jnp.exp(parts[:, 0] - top[None]), axis=0)
    return jnp.stack([top, total, jnp.sum(parts[:, 2], axis=0), jnp.sum(parts[:, 3], axis=0)])


def add_up(blocks):
    return jnp.sum(blocks.astype(jnp.float32), axis=0).astype(jnp.bfloat16)


def contract(left, right, dims):
    return lax.dot_general(left, right, (dims, ((), ())), preferred_element_type=jnp.float32)


def body(hidden, unembed, teacher, teacher_lse, cotangent):
    tokens, columns = teacher.shape
    features = unembed.shape[0]
    shard = features // (NX * NY)
    rows_a = shard - ROWS_B
    mine = hidden.T

    x = lax.axis_index("voc") // NY
    part_b = mine[:ROWS_B]
    came_from = [part_b] + [lax.ppermute(part_b, "voc", X_SHIFTS[k]) for k in range(1, NX)]
    place = lax.broadcasted_iota(jnp.int32, (NX, ROWS_B, tokens), 0)
    line = jnp.broadcast_to(came_from[-1][None], place.shape)
    for k in range(NX - 1):
        line = jnp.where(place == lax.rem(x + NX - k, NX), came_from[k][None], line)
    gathered_b = lax.all_gather(
        line.reshape(NX * ROWS_B, tokens), "voc", axis_index_groups=Y_GROUPS, axis=0, tiled=True
    )
    row = spread(mine[ROWS_B:], "voc", Y_GROUPS).reshape(NY * rows_a, tokens)
    gathered_a = spread(row, "voc", X_GROUPS).reshape(NX * NY * rows_a, tokens)

    by_shard = unembed.reshape(NX, NY, shard, columns)
    unembed_b = by_shard[:, :, :ROWS_B].transpose(1, 0, 2, 3).reshape(-1, columns)
    unembed_a = by_shard[:, :, ROWS_B:].reshape(-1, columns)
    to_x = [
        lax.dynamic_slice_in_dim(by_shard[:, :, ROWS_B:], lax.rem(x + k, NX), 1, 0).reshape(-1, columns)
        for k in range(NX)
    ]

    teacher_t = teacher.T.astype(jnp.float32)
    shifted = teacher_t - teacher_lse[None, :]
    probs = jnp.exp(shifted)
    logits = contract(unembed_b, gathered_b, ((0,), (0,))) + contract(unembed_a, gathered_a, ((0,), (0,)))
    top = jnp.max(logits, axis=0)
    total = jnp.sum(jnp.exp(logits - top[None, :]), axis=0)
    mass = jnp.sum(probs, axis=0)
    cross = jnp.sum(probs * (shifted - logits), axis=0)
    stats = jnp.stack([top, total, mass, cross])
    every = lax.all_to_all(jnp.broadcast_to(stats[None], (NX * NY,) + stats.shape), "voc", 0, 0, tiled=True)
    natural = jnp.concatenate(
        [
            gathered_b.reshape(NY, NX, ROWS_B, tokens).transpose(1, 0, 2, 3),
            gathered_a.reshape(NX, NY, rows_a, tokens),
        ],
        axis=2,
    ).reshape(NZ, NC, features // NZ // NC, tokens)
    core = lax.rem(lax.axis_index("tok"), NC)
    rows_kept = lax.dynamic_slice_in_dim(natural, core, 1, 1).reshape(-1, tokens)
    rows_given = lax.dynamic_slice_in_dim(natural, 1 - core, 1, 1).reshape(-1, tokens)
    every, rows_kept, rows_given, to_x = lax.optimization_barrier((every, rows_kept, rows_given, to_x))
    stats = merge(every)
    row_mass = stats[2]
    student_lse = stats[0] + jnp.log(stats[1])
    loss = stats[3] + row_mass * student_lse
    grad_logits = (
        cotangent[None, :] * (jnp.exp(logits - student_lse[None, :]) * row_mass[None, :] - probs)
    ).astype(jnp.bfloat16)

    given = contract(rows_given, grad_logits, ((1,), (1,))).astype(jnp.bfloat16)
    came = lax.ppermute(given, "tok", CORE_SWAP)

    terms_b = jnp.dot(unembed_b, grad_logits, preferred_element_type=jnp.float32).astype(jnp.bfloat16)
    chip_terms = (contract(rows_kept, grad_logits, ((1,), (1,))) + came.astype(jnp.float32)).astype(jnp.bfloat16)
    chip_terms, terms_b, grad_later = lax.optimization_barrier((chip_terms, terms_b, grad_logits))
    line_b = lax.psum_scatter(
        terms_b, "voc", axis_index_groups=Y_GROUPS, scatter_dimension=0, tiled=True
    )
    summed = add_up(exchange(chip_terms.reshape(NZ, -1, columns), "tok", Z_GROUPS))
    grad_unembed = lax.all_gather(summed, "tok", axis=0, tiled=True)
    row_a = jnp.dot(to_x[0], grad_later, preferred_element_type=jnp.float32)
    for k in range(1, NX):
        term = jnp.dot(to_x[k], grad_later, preferred_element_type=jnp.float32).astype(jnp.bfloat16)
        row_a = row_a + lax.ppermute(term, "voc", X_SHIFTS[k]).astype(jnp.float32)
    row_a = row_a.astype(jnp.bfloat16)
    out_a = add_up(exchange(row_a.reshape(NY, -1, tokens), "voc", Y_GROUPS))
    out_b = add_up(exchange(line_b.reshape(NX, -1, tokens), "voc", X_GROUPS))
    grad_hidden = jnp.concatenate([out_b, out_a], axis=0).T
    return (loss, grad_hidden, grad_unembed)


def solution(mesh):
    placed = (P("tok", "voc"), P(None, "voc"), P("tok", "voc"), P("tok"), P("tok"))
    return jax.shard_map(
        body,
        mesh=mesh,
        in_specs=placed,
        out_specs=(P("tok"), P("tok", "voc"), P(None, "voc")),
        check_vma=False,
    )
```

```python
import jax
import jax.numpy as jnp
from jax import lax
from jax.experimental import pallas as pl
from jax.sharding import PartitionSpec as P

NX, NY, NZ, NC = 4, 8, 8, 2
Y_GROUPS = [[x * NY + y for y in range(NY)] for x in range(NX)]
X_GROUPS = [[x * NY + y for x in range(NX)] for y in range(NY)]
Z_GROUPS = [[z * NC + c for z in range(NZ)] for c in range(NC)]
CORE_SWAP = [(z * NC + c, z * NC + 1 - c) for z in range(NZ) for c in range(NC)]
GATHER_B = 64
SCATTER_B = 80


def exchange(blocks, axis, groups):
    return lax.all_to_all(blocks, axis, 0, 0, tiled=True, axis_index_groups=groups)


def spread(block, axis, groups):
    copies = jnp.broadcast_to(block[None], (len(groups[0]),) + block.shape)
    return exchange(copies, axis, groups)


def merge(parts):
    top = jnp.max(parts[:, 0], axis=0)
    total = jnp.sum(parts[:, 1] * jnp.exp(parts[:, 0] - top[None]), axis=0)
    return jnp.stack([top, total, jnp.sum(parts[:, 2], axis=0), jnp.sum(parts[:, 3], axis=0)])


def add_up(blocks):
    return jnp.sum(blocks.astype(jnp.float32), axis=0).astype(jnp.bfloat16)


def contract(left, right, dims):
    return lax.dot_general(left, right, (dims, ((), ())), preferred_element_type=jnp.float32)


def product_kernel(left, right, out):
    out[...] = jnp.dot(left[...], right[...], preferred_element_type=jnp.float32).astype(out.dtype)


def product(left, right, rows=512):
    (count, depth), columns = left.shape, right.shape[1]
    return pl.pallas_call(
        product_kernel,
        grid=(count // rows,),
        in_specs=[
            pl.BlockSpec((rows, depth), lambda i: (i, 0)),
            pl.BlockSpec((depth, columns), lambda i: (0, 0)),
        ],
        out_specs=pl.BlockSpec((rows, columns), lambda i: (i, 0)),
        out_shape=jax.ShapeDtypeStruct((count, columns), jnp.bfloat16),
        cost_estimate=pl.CostEstimate(
            flops=2 * count * depth * columns,
            bytes_accessed=2 * (count * depth + depth * columns + count * columns),
            transcendentals=0,
        ),
    )(left, right)


def body(hidden, unembed, teacher, teacher_lse, cotangent):
    tokens, columns = teacher.shape
    features = unembed.shape[0]
    shard = features // (NX * NY)
    rows_a = shard - GATHER_B
    mine = hidden.T

    line = spread(mine[:GATHER_B], "voc", X_GROUPS).reshape(NX * GATHER_B, tokens)
    gathered_b = lax.all_gather(line, "voc", axis_index_groups=Y_GROUPS, axis=0, tiled=True)
    part_a = lax.optimization_barrier((mine[GATHER_B:], line))[0]
    row = spread(part_a, "voc", Y_GROUPS).reshape(NY * rows_a, tokens)
    gathered_a = spread(row, "voc", X_GROUPS).reshape(NX * NY * rows_a, tokens)

    by_shard = unembed.reshape(NX, NY, shard, columns)
    unembed_b = by_shard[:, :, :GATHER_B].transpose(1, 0, 2, 3).reshape(-1, columns)
    unembed_a = by_shard[:, :, GATHER_B:].reshape(-1, columns)
    scatter_b = by_shard[:, :, :SCATTER_B].transpose(1, 0, 2, 3).reshape(-1, columns)
    scatter_a = by_shard[:, :, SCATTER_B:].reshape(-1, columns)

    teacher_t = teacher.T.astype(jnp.float32)
    shifted = teacher_t - teacher_lse[None, :]
    probs = jnp.exp(shifted)
    logits = contract(unembed_b, gathered_b, ((0,), (0,))) + contract(unembed_a, gathered_a, ((0,), (0,)))
    top = jnp.max(logits, axis=0)
    total = jnp.sum(jnp.exp(logits - top[None, :]), axis=0)
    mass = jnp.sum(probs, axis=0)
    cross = jnp.sum(probs * (shifted - logits), axis=0)
    stats = jnp.stack([top, total, mass, cross])
    every = lax.all_to_all(jnp.broadcast_to(stats[None], (NX * NY,) + stats.shape), "voc", 0, 0, tiled=True)
    natural = jnp.concatenate(
        [
            gathered_b.reshape(NY, NX, GATHER_B, tokens).transpose(1, 0, 2, 3),
            gathered_a.reshape(NX, NY, rows_a, tokens),
        ],
        axis=2,
    ).reshape(NZ, NC, features // NZ // NC, tokens)
    core = lax.rem(lax.axis_index("tok"), NC)
    rows_kept = lax.dynamic_slice_in_dim(natural, core, 1, 1).reshape(-1, tokens)
    rows_given = lax.dynamic_slice_in_dim(natural, 1 - core, 1, 1).reshape(-1, tokens)
    every, rows_kept, rows_given, scatter_a, scatter_b = lax.optimization_barrier(
        (every, rows_kept, rows_given, scatter_a, scatter_b)
    )
    stats = merge(every)
    row_mass = stats[2]
    student_lse = stats[0] + jnp.log(stats[1])
    loss = stats[3] + row_mass * student_lse
    grad_logits = (
        cotangent[None, :] * (jnp.exp(logits - student_lse[None, :]) * row_mass[None, :] - probs)
    ).astype(jnp.bfloat16)

    given = contract(rows_given, grad_logits, ((1,), (1,))).astype(jnp.bfloat16)
    came = lax.ppermute(given, "tok", CORE_SWAP)

    terms_b = product(scatter_b, grad_logits)
    line_b = lax.psum_scatter(
        terms_b, "voc", axis_index_groups=Y_GROUPS, scatter_dimension=0, tiled=True
    )
    chip_terms = (contract(rows_kept, grad_logits, ((1,), (1,))) + came.astype(jnp.float32)).astype(jnp.bfloat16)
    summed = add_up(exchange(chip_terms.reshape(NZ, -1, columns), "tok", Z_GROUPS))
    grad_unembed = lax.all_gather(summed, "tok", axis=0, tiled=True)

    terms_a = product(scatter_a, grad_logits)
    row_a = add_up(exchange(terms_a.reshape(NX, -1, tokens), "voc", X_GROUPS))
    out_a = add_up(exchange(row_a.reshape(NY, -1, tokens), "voc", Y_GROUPS))
    out_b = add_up(exchange(line_b.reshape(NX, -1, tokens), "voc", X_GROUPS))
    grad_hidden = jnp.concatenate([out_b, out_a], axis=0).T
    return (loss, grad_hidden, grad_unembed)


def solution(mesh):
    placed = (P("tok", "voc"), P(None, "voc"), P("tok", "voc"), P("tok"), P("tok"))
    return jax.shard_map(
        body,
        mesh=mesh,
        in_specs=placed,
        out_specs=(P("tok"), P("tok", "voc"), P(None, "voc")),
        check_vma=False,
    )
```

```python
import jax
import jax.numpy as jnp
from jax import lax
from jax.experimental import pallas as pl
from jax.sharding import PartitionSpec as P

NX, NY, NZ, NC = 4, 8, 8, 2
Y_GROUPS = [[x * NY + y for y in range(NY)] for x in range(NX)]
X_GROUPS = [[x * NY + y for x in range(NX)] for y in range(NY)]
Z_GROUPS = [[z * NC + c for z in range(NZ)] for c in range(NC)]
CORE_SWAP = [(z * NC + c, z * NC + 1 - c) for z in range(NZ) for c in range(NC)]
GATHER_B = 64


def exchange(blocks, axis, groups):
    return lax.all_to_all(blocks, axis, 0, 0, tiled=True, axis_index_groups=groups)


def spread(block, axis, groups):
    copies = jnp.broadcast_to(block[None], (len(groups[0]),) + block.shape)
    return exchange(copies, axis, groups)


def merge(parts):
    top = jnp.max(parts[:, 0], axis=0)
    total = jnp.sum(parts[:, 1] * jnp.exp(parts[:, 0] - top[None]), axis=0)
    return jnp.stack([top, total, jnp.sum(parts[:, 2], axis=0), jnp.sum(parts[:, 3], axis=0)])


def add_up(blocks):
    return jnp.sum(blocks.astype(jnp.float32), axis=0).astype(jnp.bfloat16)


def contract(left, right, dims):
    return lax.dot_general(left, right, (dims, ((), ())), preferred_element_type=jnp.float32)


def product_kernel(left, right, out):
    out[...] = jnp.dot(left[...], right[...], preferred_element_type=jnp.float32).astype(out.dtype)


def product(left, right, rows=896):
    (count, depth), columns = left.shape, right.shape[1]
    return pl.pallas_call(
        product_kernel,
        grid=(count // rows,),
        in_specs=[
            pl.BlockSpec((rows, depth), lambda i: (i, 0)),
            pl.BlockSpec((depth, columns), lambda i: (0, 0)),
        ],
        out_specs=pl.BlockSpec((rows, columns), lambda i: (i, 0)),
        out_shape=jax.ShapeDtypeStruct((count, columns), jnp.bfloat16),
        cost_estimate=pl.CostEstimate(
            flops=2 * count * depth * columns,
            bytes_accessed=2 * (count * depth + depth * columns + count * columns),
            transcendentals=0,
        ),
    )(left, right)


def body(hidden, unembed, teacher, teacher_lse, cotangent):
    tokens, columns = teacher.shape
    features = unembed.shape[0]
    shard = features // (NX * NY)
    rows_a = shard - GATHER_B
    mine = hidden.T

    line = spread(mine[:GATHER_B], "voc", X_GROUPS).reshape(NX * GATHER_B, tokens)
    gathered_b = lax.all_gather(line, "voc", axis_index_groups=Y_GROUPS, axis=0, tiled=True)
    part_a = lax.optimization_barrier((mine[GATHER_B:], line))[0]
    row = spread(part_a, "voc", Y_GROUPS).reshape(NY * rows_a, tokens)
    gathered_a = spread(row, "voc", X_GROUPS).reshape(NX * NY * rows_a, tokens)

    by_shard = unembed.reshape(NX, NY, shard, columns)
    unembed_b = by_shard[:, :, :GATHER_B].transpose(1, 0, 2, 3).reshape(-1, columns)
    unembed_a = by_shard[:, :, GATHER_B:].reshape(-1, columns)
    by_y = by_shard.transpose(1, 0, 2, 3).reshape(features, columns)

    teacher_t = teacher.T.astype(jnp.float32)
    shifted = teacher_t - teacher_lse[None, :]
    probs = jnp.exp(shifted)
    logits = contract(unembed_b, gathered_b, ((0,), (0,))) + contract(unembed_a, gathered_a, ((0,), (0,)))
    top = jnp.max(logits, axis=0)
    total = jnp.sum(jnp.exp(logits - top[None, :]), axis=0)
    mass = jnp.sum(probs, axis=0)
    cross = jnp.sum(probs * (shifted - logits), axis=0)
    stats = jnp.stack([top, total, mass, cross])
    every = lax.all_to_all(jnp.broadcast_to(stats[None], (NX * NY,) + stats.shape), "voc", 0, 0, tiled=True)
    natural = jnp.concatenate(
        [
            gathered_b.reshape(NY, NX, GATHER_B, tokens).transpose(1, 0, 2, 3),
            gathered_a.reshape(NX, NY, rows_a, tokens),
        ],
        axis=2,
    ).reshape(NZ, NC, features // NZ // NC, tokens)
    core = lax.rem(lax.axis_index("tok"), NC)
    rows_kept = lax.dynamic_slice_in_dim(natural, core, 1, 1).reshape(-1, tokens)
    rows_given = lax.dynamic_slice_in_dim(natural, 1 - core, 1, 1).reshape(-1, tokens)
    every, rows_kept, rows_given, by_y = lax.optimization_barrier((every, rows_kept, rows_given, by_y))
    stats = merge(every)
    row_mass = stats[2]
    student_lse = stats[0] + jnp.log(stats[1])
    loss = stats[3] + row_mass * student_lse
    grad_logits = (
        cotangent[None, :] * (jnp.exp(logits - student_lse[None, :]) * row_mass[None, :] - probs)
    ).astype(jnp.bfloat16)

    given = contract(rows_given, grad_logits, ((1,), (1,))).astype(jnp.bfloat16)
    came = lax.ppermute(given, "tok", CORE_SWAP)

    grad_later = lax.optimization_barrier((grad_logits, given))[0]
    line = lax.psum_scatter(
        product(by_y, grad_later), "voc", axis_index_groups=Y_GROUPS, scatter_dimension=0, tiled=True
    )
    chip_terms = (contract(rows_kept, grad_logits, ((1,), (1,))) + came.astype(jnp.float32)).astype(jnp.bfloat16)
    summed = add_up(exchange(chip_terms.reshape(NZ, -1, columns), "tok", Z_GROUPS))
    own = spread(summed, "tok", Z_GROUPS)
    other = lax.ppermute(own, "tok", CORE_SWAP)
    line = lax.optimization_barrier((line, own))[0]
    grad_hidden = add_up(exchange(line.reshape(NX, -1, tokens), "voc", X_GROUPS)).T
    by_core = (NZ, NC) + own.shape[1:]
    mine_here = lax.broadcasted_iota(jnp.int32, by_core, 1) == core
    grad_unembed = jnp.where(mine_here, own[:, None], other[:, None]).reshape(features, columns)
    return (loss, grad_hidden, grad_unembed)


def solution(mesh):
    placed = (P("tok", "voc"), P(None, "voc"), P("tok", "voc"), P("tok"), P("tok"))
    return jax.shard_map(
        body,
        mesh=mesh,
        in_specs=placed,
        out_specs=(P("tok"), P("tok", "voc"), P(None, "voc")),
        check_vma=False,
    )
```

```python
import jax
import jax.numpy as jnp
from jax import lax
from jax.experimental import pallas as pl
from jax.sharding import PartitionSpec as P

NX, NY, NZ, NC = 4, 8, 8, 2
Y_GROUPS = [[x * NY + y for y in range(NY)] for x in range(NX)]
X_GROUPS = [[x * NY + y for x in range(NX)] for y in range(NY)]
Z_GROUPS = [[z * NC + c for z in range(NZ)] for c in range(NC)]
CORE_SWAP = [(z * NC + c, z * NC + 1 - c) for z in range(NZ) for c in range(NC)]
X_SHIFTS = [[(x * NY + y, (x + k) % NX * NY + y) for x in range(NX) for y in range(NY)] for k in range(NX)]
GATHER_B = 64


def exchange(blocks, axis, groups):
    return lax.all_to_all(blocks, axis, 0, 0, tiled=True, axis_index_groups=groups)


def spread(block, axis, groups):
    copies = jnp.broadcast_to(block[None], (len(groups[0]),) + block.shape)
    return exchange(copies, axis, groups)


def merge(parts):
    top = jnp.max(parts[:, 0], axis=0)
    total = jnp.sum(parts[:, 1] * jnp.exp(parts[:, 0] - top[None]), axis=0)
    return jnp.stack([top, total, jnp.sum(parts[:, 2], axis=0), jnp.sum(parts[:, 3], axis=0)])


def add_up(blocks):
    return jnp.sum(blocks.astype(jnp.float32), axis=0).astype(jnp.bfloat16)


def contract(left, right, dims):
    return lax.dot_general(left, right, (dims, ((), ())), preferred_element_type=jnp.float32)


def product_kernel(left, right, out):
    out[...] = jnp.dot(left[...], right[...], preferred_element_type=jnp.float32).astype(out.dtype)


def product(left, right, rows=896):
    (count, depth), columns = left.shape, right.shape[1]
    return pl.pallas_call(
        product_kernel,
        grid=(count // rows,),
        in_specs=[
            pl.BlockSpec((rows, depth), lambda i: (i, 0)),
            pl.BlockSpec((depth, columns), lambda i: (0, 0)),
        ],
        out_specs=pl.BlockSpec((rows, columns), lambda i: (i, 0)),
        out_shape=jax.ShapeDtypeStruct((count, columns), jnp.bfloat16),
        cost_estimate=pl.CostEstimate(
            flops=2 * count * depth * columns,
            bytes_accessed=2 * (count * depth + depth * columns + count * columns),
            transcendentals=0,
        ),
    )(left, right)


def body(hidden, unembed, teacher, teacher_lse, cotangent):
    tokens, columns = teacher.shape
    features = unembed.shape[0]
    shard = features // (NX * NY)
    rows_a = shard - GATHER_B
    mine = hidden.T

    line = spread(mine[:GATHER_B], "voc", X_GROUPS).reshape(NX * GATHER_B, tokens)
    gathered_b = lax.all_gather(line, "voc", axis_index_groups=Y_GROUPS, axis=0, tiled=True)
    part_a = lax.optimization_barrier((mine[GATHER_B:], line))[0]
    row = spread(part_a, "voc", Y_GROUPS).reshape(NY * rows_a, tokens)
    gathered_a = spread(row, "voc", X_GROUPS).reshape(NX * NY * rows_a, tokens)

    by_shard = unembed.reshape(NX, NY, shard, columns)
    unembed_b = by_shard[:, :, :GATHER_B].transpose(1, 0, 2, 3).reshape(-1, columns)
    unembed_a = by_shard[:, :, GATHER_B:].reshape(-1, columns)
    by_y = by_shard.transpose(1, 0, 2, 3).reshape(features, columns)

    teacher_t = teacher.T.astype(jnp.float32)
    shifted = teacher_t - teacher_lse[None, :]
    probs = jnp.exp(shifted)
    logits = contract(unembed_b, gathered_b, ((0,), (0,))) + contract(unembed_a, gathered_a, ((0,), (0,)))
    top = jnp.max(logits, axis=0)
    total = jnp.sum(jnp.exp(logits - top[None, :]), axis=0)
    mass = jnp.sum(probs, axis=0)
    cross = jnp.sum(probs * (shifted - logits), axis=0)
    stats = jnp.stack([top, total, mass, cross])
    every = lax.all_to_all(jnp.broadcast_to(stats[None], (NX * NY,) + stats.shape), "voc", 0, 0, tiled=True)
    natural = jnp.concatenate(
        [
            gathered_b.reshape(NY, NX, GATHER_B, tokens).transpose(1, 0, 2, 3),
            gathered_a.reshape(NX, NY, rows_a, tokens),
        ],
        axis=2,
    ).reshape(NZ, NC, features // NZ // NC, tokens)
    core = lax.rem(lax.axis_index("tok"), NC)
    rows_kept = lax.dynamic_slice_in_dim(natural, core, 1, 1).reshape(-1, tokens)
    rows_given = lax.dynamic_slice_in_dim(natural, 1 - core, 1, 1).reshape(-1, tokens)
    every, rows_kept, rows_given, by_y = lax.optimization_barrier((every, rows_kept, rows_given, by_y))
    stats = merge(every)
    row_mass = stats[2]
    student_lse = stats[0] + jnp.log(stats[1])
    loss = stats[3] + row_mass * student_lse
    grad_logits = (
        cotangent[None, :] * (jnp.exp(logits - student_lse[None, :]) * row_mass[None, :] - probs)
    ).astype(jnp.bfloat16)

    given = contract(rows_given, grad_logits, ((1,), (1,))).astype(jnp.bfloat16)
    came = lax.ppermute(given, "tok", CORE_SWAP)

    grad_later = lax.optimization_barrier((grad_logits, given))[0]
    line = lax.psum_scatter(
        product(by_y, grad_later), "voc", axis_index_groups=Y_GROUPS, scatter_dimension=0, tiled=True
    )
    chip_terms = (contract(rows_kept, grad_logits, ((1,), (1,))) + came.astype(jnp.float32)).astype(jnp.bfloat16)
    summed = add_up(exchange(chip_terms.reshape(NZ, -1, columns), "tok", Z_GROUPS))
    own = spread(summed, "tok", Z_GROUPS)
    x = lax.axis_index("voc") // NY
    for_x = line.reshape(NX, -1, tokens)
    blocks = [lax.dynamic_index_in_dim(for_x, lax.rem(x + k, NX), 0, False) for k in range(NX)]
    arrived = blocks[:1] + [lax.ppermute(blocks[k], "voc", X_SHIFTS[k]) for k in range(1, NX)]
    own, arrived = lax.optimization_barrier((own, arrived))
    other = lax.ppermute(own, "tok", CORE_SWAP)
    grad_hidden = sum(block.astype(jnp.float32) for block in arrived).astype(jnp.bfloat16).T
    by_core = (NZ, NC) + own.shape[1:]
    mine_here = lax.broadcasted_iota(jnp.int32, by_core, 1) == core
    grad_unembed = jnp.where(mine_here, own[:, None], other[:, None]).reshape(features, columns)
    return (loss, grad_hidden, grad_unembed)


def solution(mesh):
    placed = (P("tok", "voc"), P(None, "voc"), P("tok", "voc"), P("tok"), P("tok"))
    return jax.shard_map(
        body,
        mesh=mesh,
        in_specs=placed,
        out_specs=(P("tok"), P("tok", "voc"), P(None, "voc")),
        check_vma=False,
    )
```

```python
import jax
import jax.numpy as jnp
from jax import lax
from jax.experimental import pallas as pl
from jax.sharding import PartitionSpec as P

NX, NY, NZ, NC = 4, 8, 8, 2
Y_GROUPS = [[x * NY + y for y in range(NY)] for x in range(NX)]
X_GROUPS = [[x * NY + y for x in range(NX)] for y in range(NY)]
Z_GROUPS = [[z * NC + c for z in range(NZ)] for c in range(NC)]
CORE_SWAP = [(z * NC + c, z * NC + 1 - c) for z in range(NZ) for c in range(NC)]
X_SHIFTS = [[(x * NY + y, (x + k) % NX * NY + y) for x in range(NX) for y in range(NY)] for k in range(NX)]
GATHER_B = 64


def exchange(blocks, axis, groups):
    return lax.all_to_all(blocks, axis, 0, 0, tiled=True, axis_index_groups=groups)


def spread(block, axis, groups):
    copies = jnp.broadcast_to(block[None], (len(groups[0]),) + block.shape)
    return exchange(copies, axis, groups)


def merge(parts):
    top = jnp.max(parts[:, 0], axis=0)
    total = jnp.sum(parts[:, 1] * jnp.exp(parts[:, 0] - top[None]), axis=0)
    return jnp.stack([top, total, jnp.sum(parts[:, 2], axis=0), jnp.sum(parts[:, 3], axis=0)])


def add_up(blocks):
    return jnp.sum(blocks.astype(jnp.float32), axis=0).astype(jnp.bfloat16)


def contract(left, right, dims):
    return lax.dot_general(left, right, (dims, ((), ())), preferred_element_type=jnp.float32)


def product_kernel(left, right, out):
    out[...] = jnp.dot(left[...], right[...], preferred_element_type=jnp.float32).astype(out.dtype)


def product(left, right, rows=1792):
    (count, depth), columns = left.shape, right.shape[1]
    return pl.pallas_call(
        product_kernel,
        grid=(count // rows,),
        in_specs=[
            pl.BlockSpec((rows, depth), lambda i: (i, 0)),
            pl.BlockSpec((depth, columns), lambda i: (0, 0)),
        ],
        out_specs=pl.BlockSpec((rows, columns), lambda i: (i, 0)),
        out_shape=jax.ShapeDtypeStruct((count, columns), jnp.bfloat16),
        cost_estimate=pl.CostEstimate(
            flops=2 * count * depth * columns,
            bytes_accessed=2 * (count * depth + depth * columns + count * columns),
            transcendentals=0,
        ),
    )(left, right)


def body(hidden, unembed, teacher, teacher_lse, cotangent):
    tokens, columns = teacher.shape
    features = unembed.shape[0]
    shard = features // (NX * NY)
    rows_a = shard - GATHER_B
    mine = hidden.T

    line = spread(mine[:GATHER_B], "voc", X_GROUPS).reshape(NX * GATHER_B, tokens)
    gathered_b = lax.all_gather(line, "voc", axis_index_groups=Y_GROUPS, axis=0, tiled=True)
    part_a = lax.optimization_barrier((mine[GATHER_B:], line))[0]
    row = spread(part_a, "voc", Y_GROUPS).reshape(NY * rows_a, tokens)
    gathered_a = spread(row, "voc", X_GROUPS).reshape(NX * NY * rows_a, tokens)

    by_shard = unembed.reshape(NX, NY, shard, columns)
    unembed_b = by_shard[:, :, :GATHER_B].transpose(1, 0, 2, 3).reshape(-1, columns)
    unembed_a = by_shard[:, :, GATHER_B:].reshape(-1, columns)
    by_y = by_shard.transpose(1, 0, 2, 3).reshape(features, columns)

    teacher_t = teacher.T.astype(jnp.float32)
    shifted = teacher_t - teacher_lse[None, :]
    probs = jnp.exp(shifted)
    logits = contract(unembed_b, gathered_b, ((0,), (0,))) + contract(unembed_a, gathered_a, ((0,), (0,)))
    top = jnp.max(logits, axis=0)
    total = jnp.sum(jnp.exp(logits - top[None, :]), axis=0)
    mass = jnp.sum(probs, axis=0)
    cross = jnp.sum(probs * (shifted - logits), axis=0)
    stats = jnp.stack([top, total, mass, cross])
    every = lax.all_to_all(jnp.broadcast_to(stats[None], (NX * NY,) + stats.shape), "voc", 0, 0, tiled=True)
    natural = jnp.concatenate(
        [
            gathered_b.reshape(NY, NX, GATHER_B, tokens).transpose(1, 0, 2, 3),
            gathered_a.reshape(NX, NY, rows_a, tokens),
        ],
        axis=2,
    ).reshape(NZ, NC, features // NZ // NC, tokens)
    core = lax.rem(lax.axis_index("tok"), NC)
    rows_kept = lax.dynamic_slice_in_dim(natural, core, 1, 1).reshape(-1, tokens)
    rows_given = lax.dynamic_slice_in_dim(natural, 1 - core, 1, 1).reshape(-1, tokens)
    every, rows_kept, rows_given, by_y = lax.optimization_barrier((every, rows_kept, rows_given, by_y))
    stats = merge(every)
    row_mass = stats[2]
    student_lse = stats[0] + jnp.log(stats[1])
    loss = stats[3] + row_mass * student_lse
    grad_logits = (
        cotangent[None, :] * (jnp.exp(logits - student_lse[None, :]) * row_mass[None, :] - probs)
    ).astype(jnp.bfloat16)

    given = contract(rows_given, grad_logits, ((1,), (1,))).astype(jnp.bfloat16)
    came = lax.ppermute(given, "tok", CORE_SWAP)

    grad_later = lax.optimization_barrier((grad_logits, given))[0]
    line = lax.psum_scatter(
        product(by_y, grad_later), "voc", axis_index_groups=Y_GROUPS, scatter_dimension=0, tiled=True
    )
    chip_terms = (contract(rows_kept, grad_logits, ((1,), (1,))) + came.astype(jnp.float32)).astype(jnp.bfloat16)
    summed = add_up(exchange(chip_terms.reshape(NZ, -1, columns), "tok", Z_GROUPS))
    own = spread(summed, "tok", Z_GROUPS)
    x = lax.axis_index("voc") // NY
    for_x = line.reshape(NX, -1, tokens)
    blocks = [lax.dynamic_index_in_dim(for_x, lax.rem(x + k, NX), 0, False) for k in range(NX)]
    arrived = blocks[:1] + [lax.ppermute(blocks[k], "voc", X_SHIFTS[k]) for k in range(1, NX)]
    own, arrived = lax.optimization_barrier((own, arrived))
    other = lax.ppermute(own, "tok", CORE_SWAP)
    grad_hidden = sum(block.astype(jnp.float32) for block in arrived).astype(jnp.bfloat16).T
    by_core = (NZ, NC) + own.shape[1:]
    mine_here = lax.broadcasted_iota(jnp.int32, by_core, 1) == core
    grad_unembed = jnp.where(mine_here, own[:, None], other[:, None]).reshape(features, columns)
    return (loss, grad_hidden, grad_unembed)


def solution(mesh):
    placed = (P("tok", "voc"), P(None, "voc"), P("tok", "voc"), P("tok"), P("tok"))
    return jax.shard_map(
        body,
        mesh=mesh,
        in_specs=placed,
        out_specs=(P("tok"), P("tok", "voc"), P(None, "voc")),
        check_vma=False,
    )
```

```python
import jax
import jax.numpy as jnp
from jax import lax
from jax.experimental import pallas as pl
from jax.sharding import PartitionSpec as P

NX, NY, NZ, NC = 4, 8, 8, 2
Y_GROUPS = [[x * NY + y for y in range(NY)] for x in range(NX)]
X_GROUPS = [[x * NY + y for x in range(NX)] for y in range(NY)]
Z_GROUPS = [[z * NC + c for z in range(NZ)] for c in range(NC)]
CORE_SWAP = [(z * NC + c, z * NC + 1 - c) for z in range(NZ) for c in range(NC)]
X_SHIFTS = [[(x * NY + y, (x + k) % NX * NY + y) for x in range(NX) for y in range(NY)] for k in range(NX)]
GATHER_B = 64


def exchange(blocks, axis, groups):
    return lax.all_to_all(blocks, axis, 0, 0, tiled=True, axis_index_groups=groups)


def spread(block, axis, groups):
    copies = jnp.broadcast_to(block[None], (len(groups[0]),) + block.shape)
    return exchange(copies, axis, groups)


def merge(parts):
    top = jnp.max(parts[:, 0], axis=0)
    total = jnp.sum(parts[:, 1] * jnp.exp(parts[:, 0] - top[None]), axis=0)
    return jnp.stack([top, total, jnp.sum(parts[:, 2], axis=0), jnp.sum(parts[:, 3], axis=0)])


def add_up(blocks):
    return jnp.sum(blocks.astype(jnp.float32), axis=0).astype(jnp.bfloat16)


def contract(left, right, dims):
    return lax.dot_general(left, right, (dims, ((), ())), preferred_element_type=jnp.float32)


def product_kernel(left, right, out):
    out[...] = jnp.dot(left[...], right[...], preferred_element_type=jnp.float32).astype(out.dtype)


def product(left, right, rows=1792):
    (count, depth), columns = left.shape, right.shape[1]
    return pl.pallas_call(
        product_kernel,
        grid=(count // rows,),
        in_specs=[
            pl.BlockSpec((rows, depth), lambda i: (i, 0)),
            pl.BlockSpec((depth, columns), lambda i: (0, 0)),
        ],
        out_specs=pl.BlockSpec((rows, columns), lambda i: (i, 0)),
        out_shape=jax.ShapeDtypeStruct((count, columns), jnp.bfloat16),
        cost_estimate=pl.CostEstimate(
            flops=2 * count * depth * columns,
            bytes_accessed=2 * (count * depth + depth * columns + count * columns),
            transcendentals=0,
        ),
    )(left, right)


def stats_kernel(columns, rows, part, teacher, lse, logits, stats):
    step = pl.program_id(0)

    @pl.when(step == 0)
    def _():
        logits[...] = part[...]

    logits[...] += jnp.dot(columns[...], rows[...], preferred_element_type=jnp.float32)

    @pl.when(step == pl.num_programs(0) - 1)
    def _():
        value = logits[...]
        shifted = teacher[...].astype(jnp.float32) - lse[...]
        probs = jnp.exp(shifted)
        top = jnp.max(value, axis=0, keepdims=True)
        total = jnp.sum(jnp.exp(value - top), axis=0, keepdims=True)
        mass = jnp.sum(probs, axis=0, keepdims=True)
        cross = jnp.sum(probs * (shifted - value), axis=0, keepdims=True)
        for k, stat in enumerate((top, total, mass, cross)):
            stats[:, k, :] = jnp.broadcast_to(stat, (stats.shape[0], stats.shape[2]))


def logits_and_stats(columns, rows, part, teacher, lse, copies, depth=512):
    (count, features), tokens = columns.shape, rows.shape[1]
    whole = lambda shape: pl.BlockSpec(shape, lambda i: (0,) * len(shape))
    return pl.pallas_call(
        stats_kernel,
        grid=(features // depth,),
        in_specs=[
            pl.BlockSpec((count, depth), lambda i: (0, i)),
            pl.BlockSpec((depth, tokens), lambda i: (i, 0)),
            whole((count, tokens)),
            whole((count, tokens)),
            whole((1, tokens)),
        ],
        out_specs=[whole((count, tokens)), whole((copies, 4, tokens))],
        out_shape=[
            jax.ShapeDtypeStruct((count, tokens), jnp.float32),
            jax.ShapeDtypeStruct((copies, 4, tokens), jnp.float32),
        ],
        cost_estimate=pl.CostEstimate(
            flops=2 * count * features * tokens,
            bytes_accessed=2 * features * (count + tokens) + 12 * count * tokens,
            transcendentals=2 * count * tokens,
        ),
    )(columns, rows, part, teacher, lse)


def body(hidden, unembed, teacher, teacher_lse, cotangent):
    tokens, columns = teacher.shape
    features = unembed.shape[0]
    shard = features // (NX * NY)
    rows_a = shard - GATHER_B
    mine = hidden.T

    line = spread(mine[:GATHER_B], "voc", X_GROUPS).reshape(NX * GATHER_B, tokens)
    gathered_b = lax.all_gather(line, "voc", axis_index_groups=Y_GROUPS, axis=0, tiled=True)
    part_a = lax.optimization_barrier((mine[GATHER_B:], line))[0]
    row = spread(part_a, "voc", Y_GROUPS).reshape(NY * rows_a, tokens)
    gathered_a = spread(row, "voc", X_GROUPS).reshape(NX * NY * rows_a, tokens)

    by_shard = unembed.reshape(NX, NY, shard, columns)
    unembed_b = by_shard[:, :, :GATHER_B].transpose(1, 0, 2, 3).reshape(-1, columns)
    unembed_a = by_shard[:, :, GATHER_B:].reshape(-1, columns)
    by_y = by_shard.transpose(1, 0, 2, 3).reshape(features, columns)

    columns_b, teacher_t = lax.optimization_barrier((unembed_b.T, teacher.T))
    logits, stats = logits_and_stats(
        columns_b,
        gathered_b,
        contract(unembed_a, gathered_a, ((0,), (0,))),
        teacher_t,
        teacher_lse[None, :],
        NX * NY,
    )
    every = lax.all_to_all(stats, "voc", 0, 0, tiled=True)
    probs = jnp.exp(teacher_t.astype(jnp.float32) - teacher_lse[None, :])
    natural = jnp.concatenate(
        [
            gathered_b.reshape(NY, NX, GATHER_B, tokens).transpose(1, 0, 2, 3),
            gathered_a.reshape(NX, NY, rows_a, tokens),
        ],
        axis=2,
    ).reshape(NZ, NC, features // NZ // NC, tokens)
    core = lax.rem(lax.axis_index("tok"), NC)
    rows_kept = lax.dynamic_slice_in_dim(natural, core, 1, 1).reshape(-1, tokens)
    rows_given = lax.dynamic_slice_in_dim(natural, 1 - core, 1, 1).reshape(-1, tokens)
    every, rows_kept, rows_given, by_y = lax.optimization_barrier((every, rows_kept, rows_given, by_y))
    stats = merge(every)
    row_mass = stats[2]
    student_lse = stats[0] + jnp.log(stats[1])
    loss = stats[3] + row_mass * student_lse
    grad_logits = (
        cotangent[None, :] * (jnp.exp(logits - student_lse[None, :]) * row_mass[None, :] - probs)
    ).astype(jnp.bfloat16)

    given = contract(rows_given, grad_logits, ((1,), (1,))).astype(jnp.bfloat16)
    came = lax.ppermute(given, "tok", CORE_SWAP)

    grad_later = lax.optimization_barrier((grad_logits, given))[0]
    line = lax.psum_scatter(
        product(by_y, grad_later), "voc", axis_index_groups=Y_GROUPS, scatter_dimension=0, tiled=True
    )
    chip_terms = (contract(rows_kept, grad_logits, ((1,), (1,))) + came.astype(jnp.float32)).astype(jnp.bfloat16)
    summed = add_up(exchange(chip_terms.reshape(NZ, -1, columns), "tok", Z_GROUPS))
    own = spread(summed, "tok", Z_GROUPS)
    x = lax.axis_index("voc") // NY
    for_x = line.reshape(NX, -1, tokens)
    blocks = [lax.dynamic_index_in_dim(for_x, lax.rem(x + k, NX), 0, False) for k in range(NX)]
    arrived = blocks[:1] + [lax.ppermute(blocks[k], "voc", X_SHIFTS[k]) for k in range(1, NX)]
    own, arrived = lax.optimization_barrier((own, arrived))
    other = lax.ppermute(own, "tok", CORE_SWAP)
    grad_hidden = sum(block.astype(jnp.float32) for block in arrived).astype(jnp.bfloat16).T
    by_core = (NZ, NC) + own.shape[1:]
    mine_here = lax.broadcasted_iota(jnp.int32, by_core, 1) == core
    grad_unembed = jnp.where(mine_here, own[:, None], other[:, None]).reshape(features, columns)
    return (loss, grad_hidden, grad_unembed)


def solution(mesh):
    placed = (P("tok", "voc"), P(None, "voc"), P("tok", "voc"), P("tok"), P("tok"))
    return jax.shard_map(
        body,
        mesh=mesh,
        in_specs=placed,
        out_specs=(P("tok"), P("tok", "voc"), P(None, "voc")),
        check_vma=False,
    )
```

```python
import jax
import jax.numpy as jnp
from jax import lax
from jax.experimental import pallas as pl
from jax.sharding import PartitionSpec as P

NX, NY, NZ, NC = 4, 8, 8, 2
Y_GROUPS = [[x * NY + y for y in range(NY)] for x in range(NX)]
X_GROUPS = [[x * NY + y for x in range(NX)] for y in range(NY)]
Z_GROUPS = [[z * NC + c for z in range(NZ)] for c in range(NC)]
CORE_SWAP = [(z * NC + c, z * NC + 1 - c) for z in range(NZ) for c in range(NC)]
X_SHIFTS = [[(x * NY + y, (x + k) % NX * NY + y) for x in range(NX) for y in range(NY)] for k in range(NX)]
GATHER_B = 64


def exchange(blocks, axis, groups):
    return lax.all_to_all(blocks, axis, 0, 0, tiled=True, axis_index_groups=groups)


def spread(block, axis, groups):
    copies = jnp.broadcast_to(block[None], (len(groups[0]),) + block.shape)
    return exchange(copies, axis, groups)


def merge(parts):
    top = jnp.max(parts[:, 0], axis=0)
    total = jnp.sum(parts[:, 1] * jnp.exp(parts[:, 0] - top[None]), axis=0)
    return jnp.stack([top, total, jnp.sum(parts[:, 2], axis=0), jnp.sum(parts[:, 3], axis=0)])


def add_up(blocks):
    return jnp.sum(blocks.astype(jnp.float32), axis=0).astype(jnp.bfloat16)


def contract(left, right, dims):
    return lax.dot_general(left, right, (dims, ((), ())), preferred_element_type=jnp.float32)


def product_kernel(left, right, out):
    out[...] = jnp.dot(left[...], right[...], preferred_element_type=jnp.float32).astype(out.dtype)


def product(left, right, rows=1792):
    (count, depth), columns = left.shape, right.shape[1]
    return pl.pallas_call(
        product_kernel,
        grid=(count // rows,),
        in_specs=[
            pl.BlockSpec((rows, depth), lambda i: (i, 0)),
            pl.BlockSpec((depth, columns), lambda i: (0, 0)),
        ],
        out_specs=pl.BlockSpec((rows, columns), lambda i: (i, 0)),
        out_shape=jax.ShapeDtypeStruct((count, columns), jnp.bfloat16),
        cost_estimate=pl.CostEstimate(
            flops=2 * count * depth * columns,
            bytes_accessed=2 * (count * depth + depth * columns + count * columns),
            transcendentals=0,
        ),
    )(left, right)


def body(hidden, unembed, teacher, teacher_lse, cotangent):
    tokens, columns = teacher.shape
    features = unembed.shape[0]
    shard = features // (NX * NY)
    rows_a = shard - GATHER_B
    mine = hidden.T

    line = spread(mine[:GATHER_B], "voc", X_GROUPS).reshape(NX * GATHER_B, tokens)
    gathered_b = lax.all_gather(line, "voc", axis_index_groups=Y_GROUPS, axis=0, tiled=True)
    part_a = lax.optimization_barrier((mine[GATHER_B:], line))[0]
    row = spread(part_a, "voc", Y_GROUPS).reshape(NY * rows_a, tokens)
    gathered_a = spread(row, "voc", X_GROUPS).reshape(NX * NY * rows_a, tokens)

    by_shard = unembed.reshape(NX, NY, shard, columns)
    unembed_b = by_shard[:, :, :GATHER_B].transpose(1, 0, 2, 3).reshape(-1, columns)
    unembed_a = by_shard[:, :, GATHER_B:].reshape(-1, columns)
    by_y = by_shard.transpose(1, 0, 2, 3).reshape(features, columns)

    teacher_t = teacher.T.astype(jnp.float32)
    shifted = teacher_t - teacher_lse[None, :]
    probs = jnp.exp(shifted)
    logits = contract(unembed_b, gathered_b, ((0,), (0,))) + contract(unembed_a, gathered_a, ((0,), (0,)))
    top = jnp.max(logits, axis=0)
    total = jnp.sum(jnp.exp(logits - top[None, :]), axis=0)
    mass = jnp.sum(probs, axis=0)
    cross = jnp.sum(probs * (shifted - logits), axis=0)
    stats = jnp.stack([top, total, mass, cross])
    every = lax.all_to_all(jnp.broadcast_to(stats[None], (NX * NY,) + stats.shape), "voc", 0, 0, tiled=True)
    natural = jnp.concatenate(
        [
            gathered_b.reshape(NY, NX, GATHER_B, tokens).transpose(1, 0, 2, 3),
            gathered_a.reshape(NX, NY, rows_a, tokens),
        ],
        axis=2,
    ).reshape(NZ, NC, features // NZ // NC, tokens)
    core = lax.rem(lax.axis_index("tok"), NC)
    rows_kept = lax.dynamic_slice_in_dim(natural, core, 1, 1).reshape(-1, tokens)
    rows_given = lax.dynamic_slice_in_dim(natural, 1 - core, 1, 1).reshape(-1, tokens)
    every, rows_kept, rows_given, by_y = lax.optimization_barrier((every, rows_kept, rows_given, by_y))
    stats = merge(every)
    row_mass = stats[2]
    student_lse = stats[0] + jnp.log(stats[1])
    loss = stats[3] + row_mass * student_lse
    grad_logits = (
        cotangent[None, :] * (jnp.exp(logits - student_lse[None, :]) * row_mass[None, :] - probs)
    ).astype(jnp.bfloat16)

    given = contract(rows_given, grad_logits, ((1,), (1,))).astype(jnp.bfloat16)
    came = lax.ppermute(given, "tok", CORE_SWAP)

    grad_later = lax.optimization_barrier((grad_logits, given))[0]
    came, terms = lax.optimization_barrier((came, product(by_y, grad_later)))
    line = lax.psum_scatter(terms, "voc", axis_index_groups=Y_GROUPS, scatter_dimension=0, tiled=True)
    chip_terms = (contract(rows_kept, grad_logits, ((1,), (1,))) + came.astype(jnp.float32)).astype(jnp.bfloat16)
    summed = add_up(exchange(chip_terms.reshape(NZ, -1, columns), "tok", Z_GROUPS))
    own = spread(summed, "tok", Z_GROUPS)
    x = lax.axis_index("voc") // NY
    for_x = line.reshape(NX, -1, tokens)
    blocks = [lax.dynamic_index_in_dim(for_x, lax.rem(x + k, NX), 0, False) for k in range(NX)]
    arrived = blocks[:1] + [lax.ppermute(blocks[k], "voc", X_SHIFTS[k]) for k in range(1, NX)]
    own, arrived = lax.optimization_barrier((own, arrived))
    other = lax.ppermute(own, "tok", CORE_SWAP)
    grad_hidden = sum(block.astype(jnp.float32) for block in arrived).astype(jnp.bfloat16).T
    by_core = (NZ, NC) + own.shape[1:]
    mine_here = lax.broadcasted_iota(jnp.int32, by_core, 1) == core
    grad_unembed = jnp.where(mine_here, own[:, None], other[:, None]).reshape(features, columns)
    return (loss, grad_hidden, grad_unembed)


def solution(mesh):
    placed = (P("tok", "voc"), P(None, "voc"), P("tok", "voc"), P("tok"), P("tok"))
    return jax.shard_map(
        body,
        mesh=mesh,
        in_specs=placed,
        out_specs=(P("tok"), P("tok", "voc"), P(None, "voc")),
        check_vma=False,
    )
```

```python
import jax
import jax.numpy as jnp
from jax import lax
from jax.experimental import pallas as pl
from jax.sharding import PartitionSpec as P

NX, NY, NZ, NC = 4, 8, 8, 2
Y_GROUPS = [[x * NY + y for y in range(NY)] for x in range(NX)]
X_GROUPS = [[x * NY + y for x in range(NX)] for y in range(NY)]
Z_GROUPS = [[z * NC + c for z in range(NZ)] for c in range(NC)]
CORE_SWAP = [(z * NC + c, z * NC + 1 - c) for z in range(NZ) for c in range(NC)]
X_SHIFTS = [[(x * NY + y, (x + k) % NX * NY + y) for x in range(NX) for y in range(NY)] for k in range(NX)]
GATHER_B = 80


def exchange(blocks, axis, groups):
    return lax.all_to_all(blocks, axis, 0, 0, tiled=True, axis_index_groups=groups)


def spread(block, axis, groups):
    copies = jnp.broadcast_to(block[None], (len(groups[0]),) + block.shape)
    return exchange(copies, axis, groups)


def merge(parts):
    top = jnp.max(parts[:, 0], axis=0)
    total = jnp.sum(parts[:, 1] * jnp.exp(parts[:, 0] - top[None]), axis=0)
    return jnp.stack([top, total, jnp.sum(parts[:, 2], axis=0), jnp.sum(parts[:, 3], axis=0)])


def add_up(blocks):
    return jnp.sum(blocks.astype(jnp.float32), axis=0).astype(jnp.bfloat16)


def contract(left, right, dims):
    return lax.dot_general(left, right, (dims, ((), ())), preferred_element_type=jnp.float32)


def product_kernel(left, right, out):
    out[...] = jnp.dot(left[...], right[...], preferred_element_type=jnp.float32).astype(out.dtype)


def product(left, right, rows=1792):
    (count, depth), columns = left.shape, right.shape[1]
    return pl.pallas_call(
        product_kernel,
        grid=(count // rows,),
        in_specs=[
            pl.BlockSpec((rows, depth), lambda i: (i, 0)),
            pl.BlockSpec((depth, columns), lambda i: (0, 0)),
        ],
        out_specs=pl.BlockSpec((rows, columns), lambda i: (i, 0)),
        out_shape=jax.ShapeDtypeStruct((count, columns), jnp.bfloat16),
        cost_estimate=pl.CostEstimate(
            flops=2 * count * depth * columns,
            bytes_accessed=2 * (count * depth + depth * columns + count * columns),
            transcendentals=0,
        ),
    )(left, right)


def body(hidden, unembed, teacher, teacher_lse, cotangent):
    tokens, columns = teacher.shape
    features = unembed.shape[0]
    shard = features // (NX * NY)
    rows_a = shard - GATHER_B
    mine = hidden.T

    line = spread(mine[:GATHER_B], "voc", X_GROUPS).reshape(NX * GATHER_B, tokens)
    gathered_b = lax.all_gather(line, "voc", axis_index_groups=Y_GROUPS, axis=0, tiled=True)
    part_a = lax.optimization_barrier((mine[GATHER_B:], line))[0]
    row = spread(part_a, "voc", Y_GROUPS).reshape(NY * rows_a, tokens)
    gathered_a = spread(row, "voc", X_GROUPS).reshape(NX * NY * rows_a, tokens)

    by_shard = unembed.reshape(NX, NY, shard, columns)
    unembed_b = by_shard[:, :, :GATHER_B].transpose(1, 0, 2, 3).reshape(-1, columns)
    unembed_a = by_shard[:, :, GATHER_B:].reshape(-1, columns)
    by_y = by_shard.transpose(1, 0, 2, 3).reshape(features, columns)

    teacher_t = teacher.T.astype(jnp.float32)
    shifted = teacher_t - teacher_lse[None, :]
    probs = jnp.exp(shifted)
    logits = contract(unembed_b, gathered_b, ((0,), (0,))) + contract(unembed_a, gathered_a, ((0,), (0,)))
    top = jnp.max(logits, axis=0)
    total = jnp.sum(jnp.exp(logits - top[None, :]), axis=0)
    mass = jnp.sum(probs, axis=0)
    cross = jnp.sum(probs * (shifted - logits), axis=0)
    stats = jnp.stack([top, total, mass, cross])
    every = lax.all_to_all(jnp.broadcast_to(stats[None], (NX * NY,) + stats.shape), "voc", 0, 0, tiled=True)
    natural = jnp.concatenate(
        [
            gathered_b.reshape(NY, NX, GATHER_B, tokens).transpose(1, 0, 2, 3),
            gathered_a.reshape(NX, NY, rows_a, tokens),
        ],
        axis=2,
    ).reshape(NZ, NC, features // NZ // NC, tokens)
    core = lax.rem(lax.axis_index("tok"), NC)
    rows_kept = lax.dynamic_slice_in_dim(natural, core, 1, 1).reshape(-1, tokens)
    rows_given = lax.dynamic_slice_in_dim(natural, 1 - core, 1, 1).reshape(-1, tokens)
    every, rows_kept, rows_given, by_y = lax.optimization_barrier((every, rows_kept, rows_given, by_y))
    stats = merge(every)
    row_mass = stats[2]
    student_lse = stats[0] + jnp.log(stats[1])
    loss = stats[3] + row_mass * student_lse
    grad_logits = (
        cotangent[None, :] * (jnp.exp(logits - student_lse[None, :]) * row_mass[None, :] - probs)
    ).astype(jnp.bfloat16)

    given = contract(rows_given, grad_logits, ((1,), (1,))).astype(jnp.bfloat16)
    came = lax.ppermute(given, "tok", CORE_SWAP)

    grad_later = lax.optimization_barrier((grad_logits, given))[0]
    line = lax.psum_scatter(
        product(by_y, grad_later), "voc", axis_index_groups=Y_GROUPS, scatter_dimension=0, tiled=True
    )
    chip_terms = (contract(rows_kept, grad_logits, ((1,), (1,))) + came.astype(jnp.float32)).astype(jnp.bfloat16)
    summed = add_up(exchange(chip_terms.reshape(NZ, -1, columns), "tok", Z_GROUPS))
    own = spread(summed, "tok", Z_GROUPS)
    x = lax.axis_index("voc") // NY
    for_x = line.reshape(NX, -1, tokens)
    blocks = [lax.dynamic_index_in_dim(for_x, lax.rem(x + k, NX), 0, False) for k in range(NX)]
    arrived = blocks[:1] + [lax.ppermute(blocks[k], "voc", X_SHIFTS[k]) for k in range(1, NX)]
    own, arrived = lax.optimization_barrier((own, arrived))
    other = lax.ppermute(own, "tok", CORE_SWAP)
    grad_hidden = sum(block.astype(jnp.float32) for block in arrived).astype(jnp.bfloat16).T
    by_core = (NZ, NC) + own.shape[1:]
    mine_here = lax.broadcasted_iota(jnp.int32, by_core, 1) == core
    grad_unembed = jnp.where(mine_here, own[:, None], other[:, None]).reshape(features, columns)
    return (loss, grad_hidden, grad_unembed)


def solution(mesh):
    placed = (P("tok", "voc"), P(None, "voc"), P("tok", "voc"), P("tok"), P("tok"))
    return jax.shard_map(
        body,
        mesh=mesh,
        in_specs=placed,
        out_specs=(P("tok"), P("tok", "voc"), P(None, "voc")),
        check_vma=False,
    )
```

```python
import jax
import jax.numpy as jnp
from jax import lax
from jax.experimental import pallas as pl
from jax.sharding import PartitionSpec as P

NX, NY, NZ, NC = 4, 8, 8, 2
Y_GROUPS = [[x * NY + y for y in range(NY)] for x in range(NX)]
X_GROUPS = [[x * NY + y for x in range(NX)] for y in range(NY)]
Z_GROUPS = [[z * NC + c for z in range(NZ)] for c in range(NC)]
CORE_SWAP = [(z * NC + c, z * NC + 1 - c) for z in range(NZ) for c in range(NC)]
X_SHIFTS = [[(x * NY + y, (x + k) % NX * NY + y) for x in range(NX) for y in range(NY)] for k in range(NX)]
GATHER_B = 56


def exchange(blocks, axis, groups):
    return lax.all_to_all(blocks, axis, 0, 0, tiled=True, axis_index_groups=groups)


def spread(block, axis, groups):
    copies = jnp.broadcast_to(block[None], (len(groups[0]),) + block.shape)
    return exchange(copies, axis, groups)


def merge(parts):
    top = jnp.max(parts[:, 0], axis=0)
    total = jnp.sum(parts[:, 1] * jnp.exp(parts[:, 0] - top[None]), axis=0)
    return jnp.stack([top, total, jnp.sum(parts[:, 2], axis=0), jnp.sum(parts[:, 3], axis=0)])


def add_up(blocks):
    return jnp.sum(blocks.astype(jnp.float32), axis=0).astype(jnp.bfloat16)


def contract(left, right, dims):
    return lax.dot_general(left, right, (dims, ((), ())), preferred_element_type=jnp.float32)


def product_kernel(left, right, out):
    out[...] = jnp.dot(left[...], right[...], preferred_element_type=jnp.float32).astype(out.dtype)


def product(left, right, rows=1792):
    (count, depth), columns = left.shape, right.shape[1]
    return pl.pallas_call(
        product_kernel,
        grid=(count // rows,),
        in_specs=[
            pl.BlockSpec((rows, depth), lambda i: (i, 0)),
            pl.BlockSpec((depth, columns), lambda i: (0, 0)),
        ],
        out_specs=pl.BlockSpec((rows, columns), lambda i: (i, 0)),
        out_shape=jax.ShapeDtypeStruct((count, columns), jnp.bfloat16),
        cost_estimate=pl.CostEstimate(
            flops=2 * count * depth * columns,
            bytes_accessed=2 * (count * depth + depth * columns + count * columns),
            transcendentals=0,
        ),
    )(left, right)


def body(hidden, unembed, teacher, teacher_lse, cotangent):
    tokens, columns = teacher.shape
    features = unembed.shape[0]
    shard = features // (NX * NY)
    rows_a = shard - GATHER_B
    mine = hidden.T

    line = spread(mine[:GATHER_B], "voc", X_GROUPS).reshape(NX * GATHER_B, tokens)
    gathered_b = lax.all_gather(line, "voc", axis_index_groups=Y_GROUPS, axis=0, tiled=True)
    part_a = lax.optimization_barrier((mine[GATHER_B:], line))[0]
    row = spread(part_a, "voc", Y_GROUPS).reshape(NY * rows_a, tokens)
    gathered_a = spread(row, "voc", X_GROUPS).reshape(NX * NY * rows_a, tokens)

    by_shard = unembed.reshape(NX, NY, shard, columns)
    unembed_b = by_shard[:, :, :GATHER_B].transpose(1, 0, 2, 3).reshape(-1, columns)
    unembed_a = by_shard[:, :, GATHER_B:].reshape(-1, columns)
    by_y = by_shard.transpose(1, 0, 2, 3).reshape(features, columns)

    teacher_t = teacher.T.astype(jnp.float32)
    shifted = teacher_t - teacher_lse[None, :]
    probs = jnp.exp(shifted)
    logits = contract(unembed_b, gathered_b, ((0,), (0,))) + contract(unembed_a, gathered_a, ((0,), (0,)))
    top = jnp.max(logits, axis=0)
    total = jnp.sum(jnp.exp(logits - top[None, :]), axis=0)
    mass = jnp.sum(probs, axis=0)
    cross = jnp.sum(probs * (shifted - logits), axis=0)
    stats = jnp.stack([top, total, mass, cross])
    every = lax.all_to_all(jnp.broadcast_to(stats[None], (NX * NY,) + stats.shape), "voc", 0, 0, tiled=True)
    natural = jnp.concatenate(
        [
            gathered_b.reshape(NY, NX, GATHER_B, tokens).transpose(1, 0, 2, 3),
            gathered_a.reshape(NX, NY, rows_a, tokens),
        ],
        axis=2,
    ).reshape(NZ, NC, features // NZ // NC, tokens)
    core = lax.rem(lax.axis_index("tok"), NC)
    rows_kept = lax.dynamic_slice_in_dim(natural, core, 1, 1).reshape(-1, tokens)
    rows_given = lax.dynamic_slice_in_dim(natural, 1 - core, 1, 1).reshape(-1, tokens)
    every, rows_kept, rows_given, by_y = lax.optimization_barrier((every, rows_kept, rows_given, by_y))
    stats = merge(every)
    row_mass = stats[2]
    student_lse = stats[0] + jnp.log(stats[1])
    loss = stats[3] + row_mass * student_lse
    grad_logits = (
        cotangent[None, :] * (jnp.exp(logits - student_lse[None, :]) * row_mass[None, :] - probs)
    ).astype(jnp.bfloat16)

    given = contract(rows_given, grad_logits, ((1,), (1,))).astype(jnp.bfloat16)
    came = lax.ppermute(given, "tok", CORE_SWAP)

    grad_later = lax.optimization_barrier((grad_logits, given))[0]
    line = lax.psum_scatter(
        product(by_y, grad_later), "voc", axis_index_groups=Y_GROUPS, scatter_dimension=0, tiled=True
    )
    chip_terms = (contract(rows_kept, grad_logits, ((1,), (1,))) + came.astype(jnp.float32)).astype(jnp.bfloat16)
    summed = add_up(exchange(chip_terms.reshape(NZ, -1, columns), "tok", Z_GROUPS))
    own = spread(summed, "tok", Z_GROUPS)
    x = lax.axis_index("voc") // NY
    for_x = line.reshape(NX, -1, tokens)
    blocks = [lax.dynamic_index_in_dim(for_x, lax.rem(x + k, NX), 0, False) for k in range(NX)]
    arrived = blocks[:1] + [lax.ppermute(blocks[k], "voc", X_SHIFTS[k]) for k in range(1, NX)]
    own, arrived = lax.optimization_barrier((own, arrived))
    other = lax.ppermute(own, "tok", CORE_SWAP)
    grad_hidden = sum(block.astype(jnp.float32) for block in arrived).astype(jnp.bfloat16).T
    by_core = (NZ, NC) + own.shape[1:]
    mine_here = lax.broadcasted_iota(jnp.int32, by_core, 1) == core
    grad_unembed = jnp.where(mine_here, own[:, None], other[:, None]).reshape(features, columns)
    return (loss, grad_hidden, grad_unembed)


def solution(mesh):
    placed = (P("tok", "voc"), P(None, "voc"), P("tok", "voc"), P("tok"), P("tok"))
    return jax.shard_map(
        body,
        mesh=mesh,
        in_specs=placed,
        out_specs=(P("tok"), P("tok", "voc"), P(None, "voc")),
        check_vma=False,
    )
```
